32 devices in a mesh: vel: 4 (over y, x), space: 8 (over z, core).
Axes of the slice: x: 2, y: 2, z: 4, core: 2. Of those that a mesh axis runs over, the one named last changes fastest.
Arguments:
- distribution: float32 [2304, 32, 256], P('vel', 'space'), may hold values from -3 to 3
- moments_old: float32 [10, 32, 256], P(None, 'space'), may hold values from -6 to 6
- pore_mask: int32 [32, 256], P('space'), may hold values 0 or 1
- synthetic_rate: float32 [10], replicated, may hold values from 0.2 to 4
Outputs:
- distribution_new: float32 [2304, 32, 256], P('vel', 'space')
- moments_new: float32 [10, 32, 256], P(None, 'space')
The draws below stay inside these ranges and needn't reach their ends.
Inputs may be any that keep to these rules, and one draw needn't show every extreme that they name: `pore_mask`: 1 marks a pore cell, 0 a solid one.
All inputs are finite; a program needn't handle non-finite values. No bound on the sum of `pore_mask` on one device may be relied on, other than what follows from the above.
Results may differ from the reference program's by a relative error of at most 0.000092.
Values sent between devices are 32-bit elements; how exact they have to be, the bound alone decides.
A program may use at most 64 MiB of HBM per device.

```python
import math
import jax
import jax.numpy as jnp
from jax import lax

VX = 16
VY = 12
VZ = 12
NMOM = 10
NY = 16
NZ = 16
TSWEEPS = 2
SWEEPS = 5
VELS = 2304
NX = 32
PLANE = 256


def touch_ends(drawn, rng, low, top_value):
    dims = drawn.shape
    spot = [jax.random.randint(jax.random.fold_in(rng, axis), (), 0, dims[axis]) for axis in range(len(dims))]
    drawn = drawn.at[tuple(spot)].set(low)
    longest = dims.index(max(dims))
    spot[longest] = (spot[longest] + 1) % dims[longest]
    return drawn.at[tuple(spot)].set(top_value)


def level_of(key, shape, split, least, top_value):
    factor_of = 1.0
    for dim, parts in split:
        steps = jax.random.uniform(jax.random.fold_in(jax.random.fold_in(key, 6), dim), (parts,), jnp.float32, least / len(split), top_value / len(split))
        factor_of = factor_of * jnp.repeat(jnp.exp(steps), shape[dim] // parts).reshape((-1,) + (1,) * (len(shape) - 1 - dim))
    return factor_of


def bell_draw(stream_key, dims, deviation, most, pieces=(), held_as=jnp.bfloat16):
    entries = jax.random.normal(stream_key, dims, jnp.float32) * deviation
    if len(pieces) > 0:
        entries = level_of(stream_key, dims, pieces, -0.22, 0.18) * entries
    return jnp.clip(entries, min=-most, max=most).astype(held_as)


def setup_inputs(seed: int = 0) -> dict:
    seeds = jax.random.split(jax.random.key(seed), 5)
    return {
        "distribution": bell_draw(seeds[0], (VELS, NX, PLANE), 0.5, 3.0, ((0, 4), (1, 8)), jnp.float32),
        "moments_old": bell_draw(seeds[1], (NMOM, NX, PLANE), 1.0, 6.0, ((1, 8),), jnp.float32),
        "pore_mask": touch_ends((jax.random.randint(seeds[2], (NX, PLANE), 0, 4) < 3).astype(jnp.int32), jax.random.fold_in(seeds[2], 1), 0, 1),
        "synthetic_rate": jnp.clip(jnp.exp(jax.random.uniform(seeds[3], (NMOM,), jnp.float32, math.log(0.2), math.log(4.0))), 0.2, 4.0),
    }


extent = 3.0
collide = 1.0
coefficients = (1.0, 2.0, 2.0, 2.0, 0.6667, 0.8, 0.8, 0.8, 2.0, 2.0)


def node_values(indices, count):
    return -extent + (indices.astype(jnp.float32) + 0.5) * (2.0 * extent / count)


def velocity_tables(first_group, groups, along_x, along_y, along_z):
    first_nodes = node_values(first_group + jnp.arange(groups, dtype=jnp.int32), along_x)
    second_nodes = node_values(jnp.arange(along_y, dtype=jnp.int32), along_y)
    third_nodes = node_values(jnp.arange(along_z, dtype=jnp.int32), along_z)
    block_shape = (groups, along_y, along_z)
    speed_one = jnp.broadcast_to(first_nodes[:, None, None], block_shape).reshape(-1)
    speed_two = jnp.broadcast_to(second_nodes[None, :, None], block_shape).reshape(-1)
    speed_three = jnp.broadcast_to(third_nodes[None, None, :], block_shape).reshape(-1)
    energy = speed_one * speed_one + speed_two * speed_two + speed_three * speed_three
    functions = jnp.stack([jnp.ones_like(energy), speed_one, speed_two, speed_three, energy - 1.5,
                           speed_one * (energy - 2.5), speed_two * (energy - 2.5),
                           speed_three * (energy - 2.5), speed_one * speed_two, speed_two * speed_three])
    volume = (2.0 * extent) ** 3 / (along_x * along_y * along_z) / math.pi ** 1.5
    moment_rows = functions * volume
    factors = jnp.array(coefficients, dtype=jnp.float32)
    spread_rows = jnp.transpose(functions * factors[:, None] * jnp.exp(-energy)[None, :])
    return (speed_one, speed_two, speed_three), moment_rows, spread_rows


def upwind_sweep(padded, source, porous, speeds, along_y, along_z):
    speed_one, speed_two, speed_three = speeds
    middle = padded[:, 1:-1]
    groups, thickness, plane_cells = middle.shape
    cube_view = middle.reshape(groups, thickness, along_y, along_z)
    from_first = jnp.where(speed_one[:, None, None] > 0, padded[:, :-2], padded[:, 2:])
    from_second = jnp.where(speed_two[:, None, None, None] > 0, jnp.roll(cube_view, 1, 2), jnp.roll(cube_view, -1, 2))
    from_third = jnp.where(speed_three[:, None, None, None] > 0, jnp.roll(cube_view, 1, 3), jnp.roll(cube_view, -1, 3))
    across = jnp.abs(speed_two)[:, None, None, None] * from_second + jnp.abs(speed_three)[:, None, None, None] * from_third
    inflow = jnp.abs(speed_one)[:, None, None] * from_first + across.reshape(groups, thickness, plane_cells)
    denominator = collide + jnp.abs(speed_one) + jnp.abs(speed_two) + jnp.abs(speed_three)
    return porous[None] * (collide * source + inflow) / denominator[:, None, None]


def relax_step(padded, forcing, porous, rates, along_y, along_z):
    middle = padded[:, 1:-1]
    moment_count, thickness, plane_cells = middle.shape
    cube_view = middle.reshape(moment_count, thickness, along_y, along_z)
    beside = jnp.roll(cube_view, 1, 2) + jnp.roll(cube_view, -1, 2) + jnp.roll(cube_view, 1, 3) + jnp.roll(cube_view, -1, 3)
    neighbours = padded[:, :-2] + padded[:, 2:] + beside.reshape(moment_count, thickness, plane_cells)
    return porous[None] * (forcing + neighbours) / (rates + 6.0)[:, None, None]


def periodic_pad(field):
    return jnp.concatenate([field[:, -1:], field, field[:, :1]], axis=1)


def reference(distribution, moments_old, pore_mask, synthetic_rate):
    porous = pore_mask.astype(jnp.float32)
    speeds, moment_rows, spread_rows = velocity_tables(0, VX, VX, VY, VZ)
    velocities, planes, plane_cells = distribution.shape
    source = jnp.dot(spread_rows, moments_old.reshape(NMOM, -1), precision=lax.Precision.HIGHEST,
                     preferred_element_type=jnp.float32).reshape(distribution.shape)
    current = distribution
    for sweep_number in range(TSWEEPS):
        current = upwind_sweep(periodic_pad(current), source, porous, speeds, NY, NZ)
    moments_half = jnp.dot(moment_rows, current.reshape(velocities, -1), precision=lax.Precision.HIGHEST,
                           preferred_element_type=jnp.float32).reshape(NMOM, planes, plane_cells)
    change = moments_half - moments_old
    correction = porous[None] * change / (synthetic_rate + 6.0)[:, None, None]
    for sweep_number in range(SWEEPS - 1):
        correction = relax_step(periodic_pad(correction), change, porous, synthetic_rate, NY, NZ)
    moments_new = moments_half + correction
    lifted = jnp.dot(spread_rows, correction.reshape(NMOM, -1), precision=lax.Precision.HIGHEST,
                     preferred_element_type=jnp.float32).reshape(distribution.shape)
    distribution_new = current + porous[None] * lifted
    return distribution_new, moments_new
```

```python
import functools
import math

import jax
import jax.numpy as jnp
from jax import lax
from jax.experimental import pallas as pl
from jax.experimental.pallas import tpu as pltpu
from jax.sharding import PartitionSpec as P

VX = 16
VY = 12
VZ = 12
NY = 16
NZ = 16
TSWEEPS = 2
SWEEPS = 5

extent = 3.0
coefficients = (1.0, 2.0, 2.0, 2.0, 0.6667, 0.8, 0.8, 0.8, 2.0, 2.0)
NMOM = len(coefficients)
LANES = 128
ROWS = 8
HALF = VY // 2
CHUNK = HALF * VZ
MESH = pl.DeviceIdType.MESH


def node(index, count):
    return -extent + (index.astype(jnp.float32) + 0.5) * (2.0 * extent / count)


def node_c(k):
    return -extent + (k + 0.5) * (2.0 * extent / VZ)


def poly_parts(fields, a, b):
    k = coefficients
    q = a * a + b * b
    m = fields
    p2 = k[4] * m[4] + (k[5] * a) * m[5] + (k[6] * b) * m[6]
    p0 = (
        k[0] * m[0]
        + (k[1] * a) * m[1]
        + (k[2] * b) * m[2]
        + (k[4] * (q - 1.5)) * m[4]
        + (k[5] * a * (q - 2.5)) * m[5]
        + (k[6] * b * (q - 2.5)) * m[6]
        + (k[8] * a * b) * m[8]
    )
    p1 = k[3] * m[3] + (k[7] * (q - 2.5)) * m[7] + (k[9] * b) * m[9]
    p3 = k[7] * m[7]
    weight = jnp.exp(jnp.full((ROWS, LANES), -q, jnp.float32))
    return weight * p0, weight * p1, weight * p2, weight * p3


def poly_pair(parts, c):
    p0, p1, p2, p3 = parts
    g = math.exp(-c * c)
    even = g * p0 + (g * c * c) * p2
    odd = (g * c) * p1 + (g * c * c * c) * p3
    return even - odd, even + odd


def masks():
    lane = lax.broadcasted_iota(jnp.int32, (ROWS, LANES), 1)
    row = lax.broadcasted_iota(jnp.int32, (ROWS, LANES), 0)
    return lane, row


def from_y(f, step, lane):
    turned = pltpu.roll(f, (step * NZ) % LANES, 1)
    other = pltpu.roll(turned, ROWS // 2, 0)
    inside = (lane >= NZ) if step > 0 else (lane < LANES - NZ)
    return jnp.where(inside, turned, other)


def from_z(f, step, lane):
    near = pltpu.roll(f, step % LANES, 1)
    wrapped = pltpu.roll(f, (-step * (NZ - 1)) % LANES, 1)
    inside = (lane % NZ != 0) if step > 0 else (lane % NZ != NZ - 1)
    return jnp.where(inside, near, wrapped)


def transport_kernel(
    nvel, nspace, groups,
    f_hbm, m_ref, pore_ref, rate_ref,
    half_hbm, mnew_ref, corr_ref,
    f_ref, h_ref, g_ref, fsend, hsend, frecv, hrecv,
    acc, mrecv, pore_ext, change_ext,
    in_sem, out_sem, fs_sem, fr_sem, hs_sem, hr_sem, ms_sem, mr_sem, ps_sem, pr_sem, cs_sem, cr_sem,
):
    vel = lax.axis_index("vel")
    space = lax.axis_index("space")
    right = lax.rem(space + 1, nspace)
    left = lax.rem(space + nspace - 1, nspace)
    chunks = groups * 2
    positive = vel * 2 >= nvel
    target = jnp.where(positive, right, left)
    volume = (2.0 * extent) ** 3 / (VX * VY * VZ) / math.pi**1.5

    def load(c):
        rows = pl.ds(c * (CHUNK * ROWS), CHUNK * ROWS)
        return pltpu.make_async_copy(f_hbm.at[rows], f_ref.at[rows], in_sem.at[c])

    for c in range(chunks):
        load(c).start()

    barrier = pltpu.get_barrier_semaphore()
    for other in (left, right):
        pl.semaphore_signal(barrier, inc=1, device_id={"space": other}, device_id_type=MESH)
    for d in range(1, nvel):
        pl.semaphore_signal(
            barrier, inc=1, device_id={"vel": lax.rem(vel + d, nvel)}, device_id_type=MESH
        )

    lane, row = masks()
    plane = lax.rem(row, ROWS // 2)
    pore = pore_ref[...].astype(jnp.float32)
    pore_ext[1] = pore
    edge = jnp.where(positive, 0, ROWS // 2 - 1)
    at_edge = jnp.where(plane == edge, 1.0, 0.0)
    off_edge = 1.0 - at_edge
    acc[...] = jnp.zeros_like(acc)
    fields = [m_ref[pl.ds(m * ROWS, ROWS), :] for m in range(NMOM)]

    def upwind_x(f):
        return jnp.where(positive, pltpu.roll(f, 1, 0), pltpu.roll(f, ROWS - 1, 0))

    def pack(src, base):
        lastp = src[pl.ds(base + ROWS // 2 - 1, ROWS, stride=ROWS // 2), :]
        firstp = src[pl.ds(base, ROWS, stride=ROWS // 2), :]
        return jnp.where(positive, lastp, firstp)

    def pack_chunk(src, dst, c):
        for t in range(CHUNK // 4):
            base = pl.multiple_of(c * (CHUNK * ROWS), ROWS) + t * 4 * ROWS
            dst[pl.ds(pl.multiple_of(c * (CHUNK * 2), ROWS) + t * ROWS, ROWS), :] = pack(src, base)

    def send(src, dst, s_sem, r_sem, c):
        rows = pl.ds(c * (CHUNK * 2), CHUNK * 2)
        return pltpu.make_async_remote_copy(
            src_ref=src.at[rows], dst_ref=dst.at[rows],
            send_sem=s_sem.at[c], recv_sem=r_sem.at[c],
            device_id={"space": target}, device_id_type=MESH,
        )

    def edges(src, dst, s_sem, r_sem):
        return [
            pltpu.make_async_remote_copy(
                src_ref=src.at[1], dst_ref=dst.at[2 * (1 - s)],
                send_sem=s_sem.at[s], recv_sem=r_sem.at[s],
                device_id={"space": (left, right)[s]}, device_id_type=MESH,
            )
            for s in range(2)
        ]

    def sweep(f, src, w, amask, ab, ac, bstep, cstep):
        total = src + amask * upwind_x(f)
        total = total + ab * from_y(f, bstep, lane)
        total = total + ac * from_z(f, cstep, lane)
        return w * total

    def node_ab(group, half, jj):
        a = node(vel * groups + group, VX)
        b = node(half * HALF + jj, VY)
        return a, b

    def first_chunk(c, group, half):
        bstep = 1 if half else -1

        def body(jj, carry):
            a, b = node_ab(group, half, jj)
            abs_a, abs_b = jnp.abs(a), jnp.abs(b)
            parts = poly_parts(fields, a, b)
            amask = abs_a * off_edge
            base = (c * HALF + jj) * (VZ * ROWS)
            for k in range(VZ // 2, VZ):
                cv = node_c(k)
                src = poly_pair(parts, cv)
                w = pore / (jnp.full((ROWS, LANES), 1.0 + abs_a + abs_b, jnp.float32) + cv)
                for sign in range(2):
                    kk = k if sign else VZ - 1 - k
                    rows = pl.ds(pl.multiple_of(base, ROWS) + kk * ROWS, ROWS)
                    f = f_ref[rows, :]
                    h_ref[rows, :] = sweep(
                        f, src[sign], w, amask, abs_b, cv, bstep, 1 if sign else -1
                    )
            return carry

        lax.fori_loop(0, HALF, body, 0)

    def second_chunk(c, group, half):
        bstep = 1 if half else -1

        def body(jj, carry):
            a, b = node_ab(group, half, jj)
            abs_a, abs_b = jnp.abs(a), jnp.abs(b)
            parts = poly_parts(fields, a, b)
            amask = abs_a * off_edge
            aedge = abs_a * at_edge
            base = (c * HALF + jj) * (VZ * ROWS)
            hbase = (c * HALF + jj) * (VZ * 2)
            s0 = s1 = s2 = s3 = None
            for k in range(VZ // 2, VZ):
                cv = node_c(k)
                src = poly_pair(parts, cv)
                w = pore / (jnp.full((ROWS, LANES), 1.0 + abs_a + abs_b, jnp.float32) + cv)
                wa = w * aedge
                got = []
                for sign in range(2):
                    kk = k if sign else VZ - 1 - k
                    rows = pl.ds(pl.multiple_of(base, ROWS) + kk * ROWS, ROWS)

                    def halo(ref):
                        at = pl.multiple_of(hbase, ROWS) + kk * 2
                        lower = jnp.broadcast_to(ref[pl.ds(at, 1), :], (ROWS, LANES))
                        upper = jnp.broadcast_to(ref[pl.ds(at + 1, 1), :], (ROWS, LANES))
                        return jnp.where(row < ROWS // 2, lower, upper)

                    h = h_ref[rows, :] + wa * halo(frecv)
                    total = sweep(h, src[sign], w, amask, abs_b, cv, bstep, 1 if sign else -1)
                    total = total + wa * halo(hrecv)
                    g_ref[rows, :] = total
                    got.append(total)
                u = got[1] + got[0]
                d = got[1] - got[0]
                if s0 is None:
                    s0, s1, s2, s3 = u, cv * d, (cv * cv) * u, (cv**3) * d
                else:
                    s0, s1 = s0 + u, s1 + cv * d
                    s2, s3 = s2 + (cv * cv) * u, s3 + (cv**3) * d
            q = a * a + b * b
            heat = (q - 2.5) * s0 + s2
            terms = (
                s0, a * s0, b * s0, s1, (q - 1.5) * s0 + s2,
                a * heat, b * heat, (q - 2.5) * s1 + s3, (a * b) * s0, b * s1,
            )
            for m, term in enumerate(terms):
                rows = pl.ds(m * ROWS, ROWS)
                acc[rows, :] = acc[rows, :] + term
            return carry

        lax.fori_loop(0, HALF, body, 0)

    def store(c):
        rows = pl.ds(c * (CHUNK * ROWS), CHUNK * ROWS)
        return pltpu.make_async_copy(g_ref.at[rows], half_hbm.at[rows], out_sem.at[c])

    pl.semaphore_wait(barrier, nvel + 1)
    pores = edges(pore_ext, pore_ext, ps_sem, pr_sem)
    for copy in pores:
        copy.start()

    def phase_one(group, carry):
        for half in range(2):
            c = group * 2 + half
            load(c).wait()
            pack_chunk(f_ref, fsend, c)
            send(fsend, frecv, fs_sem, fr_sem, c).start()
            first_chunk(c, group, half)
            pack_chunk(h_ref, hsend, c)
            send(hsend, hrecv, hs_sem, hr_sem, c).start()
        return carry

    lax.fori_loop(0, groups, phase_one, 0)

    def phase_two(group, carry):
        for half in range(2):
            c = group * 2 + half
            send(fsend, frecv, fs_sem, fr_sem, c).wait_recv()
            send(hsend, hrecv, hs_sem, hr_sem, c).wait_recv()
            second_chunk(c, group, half)
            store(c).start()
        return carry

    lax.fori_loop(0, groups, phase_two, 0)

    mrecv[vel] = acc[...] * volume

    def moment_copy(d, slot):
        return pltpu.make_async_remote_copy(
            src_ref=mrecv.at[vel], dst_ref=mrecv.at[slot],
            send_sem=ms_sem.at[d - 1], recv_sem=mr_sem.at[slot],
            device_id={"vel": lax.rem(vel + d, nvel)}, device_id_type=MESH,
        )

    for d in range(1, nvel):
        moment_copy(d, vel).start()
    for d in range(1, nvel):
        moment_copy(d, lax.rem(vel + d, nvel)).wait_recv()
    total = mrecv[0]
    for s in range(1, nvel):
        total = total + mrecv[s]
    mnew_ref[...] = total
    change_ext[1] = total - m_ref[...]
    changes = edges(change_ext, change_ext, cs_sem, cr_sem)
    for copy in changes:
        copy.start()
    for copy in pores:
        copy.wait()
    for copy in changes:
        copy.wait_recv()

    first = plane == 0
    final = plane == ROWS // 2 - 1
    up = ROWS - ROWS // 2 + 1
    down = ROWS // 2 - 1
    porous = [pore_ext[s] for s in range(3)]

    def relax(m, carry):
        rows = pl.ds(pl.multiple_of(m * ROWS, ROWS), ROWS)
        scale = 1.0 / jnp.full((ROWS, LANES), rate_ref[m] + 6.0, jnp.float32)
        forcing = [change_ext[s, rows, :] for s in range(3)]
        gain = [porous[s] * scale for s in range(3)]
        value = [gain[s] * forcing[s] for s in range(3)]
        for step in range(SWEEPS - 1):
            fresh = list(value)
            for s in (range(3) if step < SWEEPS - 2 else (1,)):
                v = value[s]
                before = pltpu.roll(v, 1, 0)
                after = pltpu.roll(v, ROWS - 1, 0)
                if s > 0:
                    before = jnp.where(first, pltpu.roll(value[s - 1], up, 0), before)
                if s < 2:
                    after = jnp.where(final, pltpu.roll(value[s + 1], down, 0), after)
                beside = from_y(v, 1, lane) + from_y(v, -1, lane)
                beside = beside + from_z(v, 1, lane) + from_z(v, -1, lane)
                fresh[s] = gain[s] * (forcing[s] + (before + after + beside))
            value = fresh
        mnew_ref[rows, :] = mnew_ref[rows, :] + value[1]
        corr_ref[rows, :] = value[1]
        return carry

    lax.fori_loop(0, NMOM, relax, 0)

    for copy in changes:
        copy.wait_send()
    for d in range(1, nvel):
        moment_copy(d, vel).wait_send()

    def finish(c, carry):
        send(fsend, frecv, fs_sem, fr_sem, c).wait_send()
        send(hsend, hrecv, hs_sem, hr_sem, c).wait_send()
        store(c).wait()
        return carry

    lax.fori_loop(0, chunks, finish, 0)


def lift_kernel(groups, half_ref, corr_ref, pore_ref, out_ref):
    step = pl.program_id(0)
    vel = lax.axis_index("vel")
    pore = pore_ref[...].astype(jnp.float32)
    fields = [pore * corr_ref[pl.ds(m * ROWS, ROWS), :] for m in range(NMOM)]

    def body(jj, carry):
        a = node(vel * groups + step // 2, VX)
        b = node(lax.rem(step, 2) * HALF + jj, VY)
        parts = poly_parts(fields, a, b)
        base = pl.multiple_of(jj * (VZ * ROWS), ROWS)
        for k in range(VZ // 2, VZ):
            lifted = poly_pair(parts, node_c(k))
            for sign in range(2):
                kk = k if sign else VZ - 1 - k
                rows = pl.ds(base + kk * ROWS, ROWS)
                out_ref[rows, :] = half_ref[rows, :] + lifted[sign]
        return carry

    lax.fori_loop(0, HALF, body, 0)


def to_rows(x):
    lead, thickness, cells = x.shape
    parts = cells // LANES
    return x.reshape(lead, thickness, parts, LANES).transpose(0, 2, 1, 3).reshape(-1, LANES)


def from_rows(x, lead, thickness, cells):
    parts = cells // LANES
    return x.reshape(lead, parts, thickness, LANES).transpose(0, 2, 1, 3).reshape(lead, thickness, cells)


def body(nvel, nspace, distribution, moments_old, pore_mask, synthetic_rate):
    velocities, thickness, cells = distribution.shape
    groups = velocities // (VY * VZ)
    assert thickness * cells == ROWS * LANES and nvel % 2 == 0 and thickness >= SWEEPS - 1
    rows = to_rows(distribution)
    old = to_rows(moments_old)
    pore = to_rows(pore_mask[None])
    chunks = groups * 2
    total = velocities * ROWS
    vmem = pl.BlockSpec(memory_space=pltpu.VMEM)
    anyspace = pl.BlockSpec(memory_space=pl.ANY)
    f32 = jnp.float32
    dma = pltpu.SemaphoreType.DMA
    half, moments_new, correction = pl.pallas_call(
        functools.partial(transport_kernel, nvel, nspace, groups),
        out_shape=(
            jax.ShapeDtypeStruct((total, LANES), f32),
            jax.ShapeDtypeStruct((NMOM * ROWS, LANES), f32),
            jax.ShapeDtypeStruct((NMOM * ROWS, LANES), f32),
        ),
        in_specs=[anyspace, vmem, vmem, pl.BlockSpec(memory_space=pltpu.SMEM)],
        out_specs=(anyspace, vmem, vmem),
        scratch_shapes=[
            pltpu.VMEM((total, LANES), f32),
            pltpu.VMEM((total, LANES), f32),
            pltpu.VMEM((total, LANES), f32),
            pltpu.VMEM((velocities * 2, LANES), f32),
            pltpu.VMEM((velocities * 2, LANES), f32),
            pltpu.VMEM((velocities * 2, LANES), f32),
            pltpu.VMEM((velocities * 2, LANES), f32),
            pltpu.VMEM((NMOM * ROWS, LANES), f32),
            pltpu.VMEM((nvel, NMOM * ROWS, LANES), f32),
            pltpu.VMEM((3, ROWS, LANES), f32),
            pltpu.VMEM((3, NMOM * ROWS, LANES), f32),
            dma((chunks,)), dma((chunks,)), dma((chunks,)), dma((chunks,)), dma((chunks,)), dma((chunks,)),
            dma((nvel - 1,)), dma((nvel,)), dma((2,)), dma((2,)), dma((2,)), dma((2,)),
        ],
        compiler_params=pltpu.CompilerParams(
            collective_id=0, has_side_effects=True, vmem_limit_bytes=24 * 1024 * 1024
        ),
        name="transport",
    )(rows, old, pore, synthetic_rate)
    fixed = lambda c: (0, 0)
    moving = pl.BlockSpec((CHUNK * ROWS, LANES), lambda c: (c, 0))
    new = pl.pallas_call(
        functools.partial(lift_kernel, groups),
        out_shape=jax.ShapeDtypeStruct((total, LANES), f32),
        grid=(chunks,),
        in_specs=[
            moving,
            pl.BlockSpec((NMOM * ROWS, LANES), fixed),
            pl.BlockSpec((ROWS, LANES), fixed),
        ],
        out_specs=moving,
        name="lift",
    )(half, correction, pore)
    return (
        from_rows(new, velocities, thickness, cells),
        from_rows(moments_new, NMOM, thickness, cells),
    )


def solution(mesh):
    placed = (P("vel", "space", None), P(None, "space", None), P("space", None), P())
    return jax.shard_map(
        functools.partial(body, mesh.shape["vel"], mesh.shape["space"]),
        mesh=mesh,
        in_specs=placed,
        out_specs=(P("vel", "space", None), P(None, "space", None)),
        check_vma=False,
    )
```

```python
import functools
import math

import jax
import jax.numpy as jnp
from jax import lax
from jax.experimental import pallas as pl
from jax.experimental.pallas import tpu as pltpu
from jax.sharding import PartitionSpec as P

VX = 16
VY = 12
VZ = 12
NY = 16
NZ = 16
TSWEEPS = 2
SWEEPS = 5

extent = 3.0
coefficients = (1.0, 2.0, 2.0, 2.0, 0.6667, 0.8, 0.8, 0.8, 2.0, 2.0)
NMOM = len(coefficients)
LANES = 128
ROWS = 8
HALF = VY // 2
CHUNK = HALF * VZ
MESH = pl.DeviceIdType.MESH


def node(index, count):
    return -extent + (index.astype(jnp.float32) + 0.5) * (2.0 * extent / count)


def node_c(k):
    return -extent + (k + 0.5) * (2.0 * extent / VZ)


def poly_parts(fields, a, b):
    k = coefficients
    q = a * a + b * b
    m = fields
    p2 = k[4] * m[4] + (k[5] * a) * m[5] + (k[6] * b) * m[6]
    p0 = (
        k[0] * m[0]
        + (k[1] * a) * m[1]
        + (k[2] * b) * m[2]
        + (k[4] * (q - 1.5)) * m[4]
        + (k[5] * a * (q - 2.5)) * m[5]
        + (k[6] * b * (q - 2.5)) * m[6]
        + (k[8] * a * b) * m[8]
    )
    p1 = k[3] * m[3] + (k[7] * (q - 2.5)) * m[7] + (k[9] * b) * m[9]
    p3 = k[7] * m[7]
    weight = jnp.exp(jnp.full((ROWS, LANES), -q, jnp.float32))
    return weight * p0, weight * p1, weight * p2, weight * p3


def poly_pair(parts, c):
    p0, p1, p2, p3 = parts
    g = math.exp(-c * c)
    even = g * p0 + (g * c * c) * p2
    odd = (g * c) * p1 + (g * c * c * c) * p3
    return even - odd, even + odd


def masks():
    lane = lax.broadcasted_iota(jnp.int32, (ROWS, LANES), 1)
    row = lax.broadcasted_iota(jnp.int32, (ROWS, LANES), 0)
    return lane, row


def from_y(f, step, lane):
    turned = pltpu.roll(f, (step * NZ) % LANES, 1)
    other = pltpu.roll(turned, ROWS // 2, 0)
    inside = (lane >= NZ) if step > 0 else (lane < LANES - NZ)
    return jnp.where(inside, turned, other)


def from_z(f, step, lane):
    near = pltpu.roll(f, step % LANES, 1)
    wrapped = pltpu.roll(f, (-step * (NZ - 1)) % LANES, 1)
    inside = (lane % NZ != 0) if step > 0 else (lane % NZ != NZ - 1)
    return jnp.where(inside, near, wrapped)


def transport_kernel(
    nvel, nspace, groups,
    f_hbm, m_hbm, pore_hbm, rate_hbm,
    g_ref, mnew_ref, corr_ref,
    f_ref, h_ref, m_ref, pore_ref, rate_ref, fsend, hsend, frecv, hrecv,
    acc, mrecv, pore_ext, change_ext,
    in_sem, small_sem, fs_sem, fr_sem, hs_sem, hr_sem, ms_sem, mr_sem, ps_sem, pr_sem, cs_sem, cr_sem,
):
    vel = lax.axis_index("vel")
    space = lax.axis_index("space")
    right = lax.rem(space + 1, nspace)
    left = lax.rem(space + nspace - 1, nspace)
    chunks = groups * 2
    positive = vel * 2 >= nvel
    target = jnp.where(positive, right, left)
    volume = (2.0 * extent) ** 3 / (VX * VY * VZ) / math.pi**1.5

    def load(c):
        rows = pl.ds(c * (CHUNK * ROWS), CHUNK * ROWS)
        return pltpu.make_async_copy(f_hbm.at[rows], f_ref.at[rows], in_sem.at[c])

    small = [
        pltpu.make_async_copy(src, dst, small_sem.at[n])
        for n, (src, dst) in enumerate(
            ((m_hbm, m_ref), (pore_hbm, pore_ref), (rate_hbm, rate_ref))
        )
    ]
    for c in range(chunks):
        load(c).start()
    for copy in small:
        copy.start()

    barrier = pltpu.get_barrier_semaphore()
    for other in (left, right):
        pl.semaphore_signal(barrier, inc=1, device_id={"space": other}, device_id_type=MESH)
    for d in range(1, nvel):
        pl.semaphore_signal(
            barrier, inc=1, device_id={"vel": lax.rem(vel + d, nvel)}, device_id_type=MESH
        )

    lane, row = masks()
    plane = lax.rem(row, ROWS // 2)
    for copy in small:
        copy.wait()
    pore = pore_ref[...].astype(jnp.float32)
    pore_ext[1] = pore
    edge = jnp.where(positive, 0, ROWS // 2 - 1)
    at_edge = jnp.where(plane == edge, 1.0, 0.0)
    off_edge = 1.0 - at_edge
    acc[...] = jnp.zeros_like(acc)
    fields = [m_ref[pl.ds(m * ROWS, ROWS), :] for m in range(NMOM)]

    def upwind_x(f):
        return jnp.where(positive, pltpu.roll(f, 1, 0), pltpu.roll(f, ROWS - 1, 0))

    def pack(src, base):
        lastp = src[pl.ds(base + ROWS // 2 - 1, ROWS, stride=ROWS // 2), :]
        firstp = src[pl.ds(base, ROWS, stride=ROWS // 2), :]
        return jnp.where(positive, lastp, firstp)

    def pack_chunk(src, dst, c):
        for t in range(CHUNK // 4):
            base = pl.multiple_of(c * (CHUNK * ROWS), ROWS) + t * 4 * ROWS
            dst[pl.ds(pl.multiple_of(c * (CHUNK * 2), ROWS) + t * ROWS, ROWS), :] = pack(src, base)

    def send(src, dst, s_sem, r_sem, c):
        rows = pl.ds(c * (CHUNK * 2), CHUNK * 2)
        return pltpu.make_async_remote_copy(
            src_ref=src.at[rows], dst_ref=dst.at[rows],
            send_sem=s_sem.at[c], recv_sem=r_sem.at[c],
            device_id={"space": target}, device_id_type=MESH,
        )

    def edges(src, dst, s_sem, r_sem):
        return [
            pltpu.make_async_remote_copy(
                src_ref=src.at[1], dst_ref=dst.at[2 * (1 - s)],
                send_sem=s_sem.at[s], recv_sem=r_sem.at[s],
                device_id={"space": (left, right)[s]}, device_id_type=MESH,
            )
            for s in range(2)
        ]

    def sweep(f, src, w, amask, ab, ac, bstep, cstep):
        total = src + amask * upwind_x(f)
        total = total + ab * from_y(f, bstep, lane)
        total = total + ac * from_z(f, cstep, lane)
        return w * total

    def node_ab(group, half, jj):
        a = node(vel * groups + group, VX)
        b = node(half * HALF + jj, VY)
        return a, b

    def first_chunk(c, group, half):
        bstep = 1 if half else -1

        def body(jj, carry):
            a, b = node_ab(group, half, jj)
            abs_a, abs_b = jnp.abs(a), jnp.abs(b)
            parts = poly_parts(fields, a, b)
            amask = abs_a * off_edge
            base = (c * HALF + jj) * (VZ * ROWS)
            for k in range(VZ // 2, VZ):
                cv = node_c(k)
                src = poly_pair(parts, cv)
                w = pore / (jnp.full((ROWS, LANES), 1.0 + abs_a + abs_b, jnp.float32) + cv)
                for sign in range(2):
                    kk = k if sign else VZ - 1 - k
                    rows = pl.ds(pl.multiple_of(base, ROWS) + kk * ROWS, ROWS)
                    f = f_ref[rows, :]
                    h_ref[rows, :] = sweep(
                        f, src[sign], w, amask, abs_b, cv, bstep, 1 if sign else -1
                    )
            return carry

        lax.fori_loop(0, HALF, body, 0)

    def second_chunk(c, group, half):
        bstep = 1 if half else -1

        def body(jj, carry):
            a, b = node_ab(group, half, jj)
            abs_a, abs_b = jnp.abs(a), jnp.abs(b)
            parts = poly_parts(fields, a, b)
            amask = abs_a * off_edge
            aedge = abs_a * at_edge
            base = (c * HALF + jj) * (VZ * ROWS)
            hbase = (c * HALF + jj) * (VZ * 2)
            s0 = s1 = s2 = s3 = None
            for k in range(VZ // 2, VZ):
                cv = node_c(k)
                src = poly_pair(parts, cv)
                w = pore / (jnp.full((ROWS, LANES), 1.0 + abs_a + abs_b, jnp.float32) + cv)
                wa = w * aedge
                got = []
                for sign in range(2):
                    kk = k if sign else VZ - 1 - k
                    rows = pl.ds(pl.multiple_of(base, ROWS) + kk * ROWS, ROWS)

                    def halo(ref):
                        at = pl.multiple_of(hbase, ROWS) + kk * 2
                        lower = jnp.broadcast_to(ref[pl.ds(at, 1), :], (ROWS, LANES))
                        upper = jnp.broadcast_to(ref[pl.ds(at + 1, 1), :], (ROWS, LANES))
                        return jnp.where(row < ROWS // 2, lower, upper)

                    h = h_ref[rows, :] + wa * halo(frecv)
                    total = sweep(h, src[sign], w, amask, abs_b, cv, bstep, 1 if sign else -1)
                    total = total + wa * halo(hrecv)
                    g_ref[rows, :] = total
                    got.append(total)
                u = got[1] + got[0]
                d = got[1] - got[0]
                if s0 is None:
                    s0, s1, s2, s3 = u, cv * d, (cv * cv) * u, (cv**3) * d
                else:
                    s0, s1 = s0 + u, s1 + cv * d
                    s2, s3 = s2 + (cv * cv) * u, s3 + (cv**3) * d
            q = a * a + b * b
            heat = (q - 2.5) * s0 + s2
            terms = (
                s0, a * s0, b * s0, s1, (q - 1.5) * s0 + s2,
                a * heat, b * heat, (q - 2.5) * s1 + s3, (a * b) * s0, b * s1,
            )
            for m, term in enumerate(terms):
                rows = pl.ds(m * ROWS, ROWS)
                acc[rows, :] = acc[rows, :] + term
            return carry

        lax.fori_loop(0, HALF, body, 0)

    def prepare(c, carry):
        load(c).wait()
        pack_chunk(f_ref, fsend, c)
        return carry

    lax.fori_loop(0, chunks, prepare, 0)

    pl.semaphore_wait(barrier, nvel + 1)

    def send_first(c, carry):
        send(fsend, frecv, fs_sem, fr_sem, c).start()
        return carry

    lax.fori_loop(0, chunks, send_first, 0)
    pores = edges(pore_ext, pore_ext, ps_sem, pr_sem)
    for copy in pores:
        copy.start()

    def phase_one(group, carry):
        for half in range(2):
            c = group * 2 + half
            first_chunk(c, group, half)
            pack_chunk(h_ref, hsend, c)
            send(hsend, hrecv, hs_sem, hr_sem, c).start()
        return carry

    lax.fori_loop(0, groups, phase_one, 0)

    def phase_two(group, carry):
        for half in range(2):
            c = group * 2 + half
            send(fsend, frecv, fs_sem, fr_sem, c).wait_recv()
            send(hsend, hrecv, hs_sem, hr_sem, c).wait_recv()
            second_chunk(c, group, half)
        return carry

    lax.fori_loop(0, groups, phase_two, 0)

    mrecv[vel] = acc[...] * volume

    def moment_copy(d, slot):
        return pltpu.make_async_remote_copy(
            src_ref=mrecv.at[vel], dst_ref=mrecv.at[slot],
            send_sem=ms_sem.at[d - 1], recv_sem=mr_sem.at[slot],
            device_id={"vel": lax.rem(vel + d, nvel)}, device_id_type=MESH,
        )

    for d in range(1, nvel):
        moment_copy(d, vel).start()
    for d in range(1, nvel):
        moment_copy(d, lax.rem(vel + d, nvel)).wait_recv()
    total = mrecv[0]
    for s in range(1, nvel):
        total = total + mrecv[s]
    mnew_ref[...] = total
    change_ext[1] = total - m_ref[...]
    changes = edges(change_ext, change_ext, cs_sem, cr_sem)
    for copy in changes:
        copy.start()
    for copy in pores:
        copy.wait()
    for copy in changes:
        copy.wait_recv()

    first = plane == 0
    final = plane == ROWS // 2 - 1
    up = ROWS - ROWS // 2 + 1
    down = ROWS // 2 - 1
    porous = [pore_ext[s] for s in range(3)]

    for m in range(NMOM):
        rows = pl.ds(m * ROWS, ROWS)
        scale = 1.0 / jnp.full((ROWS, LANES), rate_ref[m] + 6.0, jnp.float32)
        forcing = [change_ext[s, rows, :] for s in range(3)]
        gain = [porous[s] * scale for s in range(3)]
        value = [gain[s] * forcing[s] for s in range(3)]
        for step in range(SWEEPS - 1):
            fresh = list(value)
            for s in (range(3) if step < SWEEPS - 2 else (1,)):
                v = value[s]
                before = pltpu.roll(v, 1, 0)
                after = pltpu.roll(v, ROWS - 1, 0)
                if s > 0:
                    before = jnp.where(first, pltpu.roll(value[s - 1], up, 0), before)
                if s < 2:
                    after = jnp.where(final, pltpu.roll(value[s + 1], down, 0), after)
                beside = from_y(v, 1, lane) + from_y(v, -1, lane)
                beside = beside + from_z(v, 1, lane) + from_z(v, -1, lane)
                fresh[s] = gain[s] * (forcing[s] + (before + after + beside))
            value = fresh
        mnew_ref[rows, :] = mnew_ref[rows, :] + value[1]
        corr_ref[rows, :] = pore * value[1]

    for copy in changes:
        copy.wait_send()
    for d in range(1, nvel):
        moment_copy(d, vel).wait_send()

    def finish(c, carry):
        send(fsend, frecv, fs_sem, fr_sem, c).wait_send()
        send(hsend, hrecv, hs_sem, hr_sem, c).wait_send()
        return carry

    lax.fori_loop(0, chunks, finish, 0)


def group_parts(m, a):
    k = coefficients
    a = jnp.full((ROWS, LANES), a, jnp.float32)
    a2 = a * a
    weight = jnp.exp(-a2)
    bb = k[4] * m[4] + (k[5] * a) * m[5]
    one = k[0] * m[0] + (k[1] * a) * m[1] + (k[4] * (a2 - 1.5)) * m[4] + (k[5] * a * (a2 - 2.5)) * m[5]
    b1 = k[2] * m[2] + (k[6] * (a2 - 2.5)) * m[6] + (k[8] * a) * m[8]
    c1 = k[3] * m[3] + (k[7] * (a2 - 2.5)) * m[7]
    return [weight * x for x in (one, b1, bb, k[6] * m[6], c1, k[9] * m[9], k[7] * m[7])]


def pair_parts(parts, b):
    one, b1, bb, bbb, c1, cb, cbb = parts
    g = math.exp(-b * b)
    p0e, p0o = g * one + (g * b * b) * bb, (g * b) * b1 + (g * b**3) * bbb
    p1e, p1o = g * c1 + (g * b * b) * cbb, (g * b) * cb
    p2e, p2o = g * bb, (g * b) * bbb
    p3 = g * cbb
    return (
        (p0e - p0o, p1e - p1o, p2e - p2o, p3),
        (p0e + p0o, p1e + p1o, p2e + p2o, p3),
    )


def node_b(j):
    return -extent + (j + 0.5) * (2.0 * extent / VY)


def lift_kernel(groups, half_ref, corr_ref, mnew_ref, out_hbm, mout_hbm, stage, sem, msem):
    vel = lax.axis_index("vel")
    size = VY * VZ * ROWS
    moments = pltpu.make_async_copy(mnew_ref, mout_hbm, msem)
    moments.start()

    def store(g):
        rows = pl.ds(g * size, size)
        return pltpu.make_async_copy(stage.at[rows], out_hbm.at[rows], sem.at[g])

    def body(g, carry):
        fields = [corr_ref[pl.ds(m * ROWS, ROWS), :] for m in range(NMOM)]
        parts = group_parts(fields, node(vel * groups + g, VX))
        base = pl.multiple_of(g * size, ROWS)
        for j in range(HALF, VY):
            both = pair_parts(parts, node_b(j))
            for bsign in range(2):
                jj = j if bsign else VY - 1 - j
                for k in range(VZ // 2, VZ):
                    lifted = poly_pair(both[bsign], node_c(k))
                    for sign in range(2):
                        kk = k if sign else VZ - 1 - k
                        rows = pl.ds(base + (jj * VZ + kk) * ROWS, ROWS)
                        stage[rows, :] = half_ref[rows, :] + lifted[sign]
        store(g).start()
        return carry

    lax.fori_loop(0, groups, body, 0)

    def finish(g, carry):
        store(g).wait()
        return carry

    lax.fori_loop(0, groups, finish, 0)
    moments.wait()


def to_rows(x):
    lead, thickness, cells = x.shape
    parts = cells // LANES
    return x.reshape(lead, thickness, parts, LANES).transpose(0, 2, 1, 3).reshape(-1, LANES)


def from_rows(x, lead, thickness, cells):
    parts = cells // LANES
    return x.reshape(lead, parts, thickness, LANES).transpose(0, 2, 1, 3).reshape(lead, thickness, cells)


def body(nvel, nspace, distribution, moments_old, pore_mask, synthetic_rate):
    velocities, thickness, cells = distribution.shape
    groups = velocities // (VY * VZ)
    assert thickness * cells == ROWS * LANES and nvel % 2 == 0 and thickness >= SWEEPS - 1
    rows = to_rows(distribution)
    old = to_rows(moments_old)
    pore = to_rows(pore_mask[None])
    chunks = groups * 2
    total = velocities * ROWS
    vmem = pl.BlockSpec(memory_space=pltpu.VMEM)
    hbm = pl.BlockSpec(memory_space=pltpu.HBM)
    f32 = jnp.float32
    dma = pltpu.SemaphoreType.DMA
    half, moments_new, correction = pl.pallas_call(
        functools.partial(transport_kernel, nvel, nspace, groups),
        out_shape=(
            jax.ShapeDtypeStruct((total, LANES), f32),
            jax.ShapeDtypeStruct((NMOM * ROWS, LANES), f32),
            jax.ShapeDtypeStruct((NMOM * ROWS, LANES), f32),
        ),
        in_specs=[hbm] * 4,
        out_specs=(vmem,) * 3,
        scratch_shapes=[
            pltpu.VMEM((total, LANES), f32),
            pltpu.VMEM((total, LANES), f32),
            pltpu.VMEM((NMOM * ROWS, LANES), f32),
            pltpu.VMEM((ROWS, LANES), jnp.int32),
            pltpu.SMEM((NMOM,), f32),
            pltpu.VMEM((velocities * 2, LANES), f32),
            pltpu.VMEM((velocities * 2, LANES), f32),
            pltpu.VMEM((velocities * 2, LANES), f32),
            pltpu.VMEM((velocities * 2, LANES), f32),
            pltpu.VMEM((NMOM * ROWS, LANES), f32),
            pltpu.VMEM((nvel, NMOM * ROWS, LANES), f32),
            pltpu.VMEM((3, ROWS, LANES), f32),
            pltpu.VMEM((3, NMOM * ROWS, LANES), f32),
            dma((chunks,)), dma((3,)), dma((chunks,)), dma((chunks,)), dma((chunks,)), dma((chunks,)),
            dma((nvel - 1,)), dma((nvel,)), dma((2,)), dma((2,)), dma((2,)), dma((2,)),
        ],
        compiler_params=pltpu.CompilerParams(
            collective_id=0, has_side_effects=True, vmem_limit_bytes=24 * 1024 * 1024
        ),
        name="transport",
    )(rows, old, pore, synthetic_rate)
    new, moments_out = pl.pallas_call(
        functools.partial(lift_kernel, groups),
        out_shape=(
            jax.ShapeDtypeStruct((total, LANES), f32),
            jax.ShapeDtypeStruct((NMOM * ROWS, LANES), f32),
        ),
        in_specs=[vmem] * 3,
        out_specs=(hbm,) * 2,
        scratch_shapes=[pltpu.VMEM((total, LANES), f32), dma((groups,)), dma(())],
        compiler_params=pltpu.CompilerParams(vmem_limit_bytes=12 * 1024 * 1024),
        name="lift",
    )(half, correction, moments_new)
    return (
        from_rows(new, velocities, thickness, cells),
        from_rows(moments_out, NMOM, thickness, cells),
    )


def solution(mesh):
    placed = (P("vel", "space", None), P(None, "space", None), P("space", None), P())
    return jax.shard_map(
        functools.partial(body, mesh.shape["vel"], mesh.shape["space"]),
        mesh=mesh,
        in_specs=placed,
        out_specs=(P("vel", "space", None), P(None, "space", None)),
        check_vma=False,
    )
```

```python
import functools
import math

import jax
import jax.numpy as jnp
from jax import lax
from jax.experimental import pallas as pl
from jax.experimental.pallas import tpu as pltpu
from jax.sharding import PartitionSpec as P

VX = 16
VY = 12
VZ = 12
NY = 16
NZ = 16
TSWEEPS = 2
SWEEPS = 5

extent = 3.0
coefficients = (1.0, 2.0, 2.0, 2.0, 0.6667, 0.8, 0.8, 0.8, 2.0, 2.0)
NMOM = len(coefficients)
LANES = 128
ROWS = 8
HALF = VY // 2
CHUNK = HALF * VZ
MESH = pl.DeviceIdType.MESH


def node(index, count):
    return -extent + (index.astype(jnp.float32) + 0.5) * (2.0 * extent / count)


def node_c(k):
    return -extent + (k + 0.5) * (2.0 * extent / VZ)


def poly_parts(fields, a, b):
    k = coefficients
    q = a * a + b * b
    m = fields
    p2 = k[4] * m[4] + (k[5] * a) * m[5] + (k[6] * b) * m[6]
    p0 = (
        k[0] * m[0]
        + (k[1] * a) * m[1]
        + (k[2] * b) * m[2]
        + (k[4] * (q - 1.5)) * m[4]
        + (k[5] * a * (q - 2.5)) * m[5]
        + (k[6] * b * (q - 2.5)) * m[6]
        + (k[8] * a * b) * m[8]
    )
    p1 = k[3] * m[3] + (k[7] * (q - 2.5)) * m[7] + (k[9] * b) * m[9]
    p3 = k[7] * m[7]
    weight = jnp.exp(jnp.full((ROWS, LANES), -q, jnp.float32))
    return weight * p0, weight * p1, weight * p2, weight * p3


def poly_pair(parts, c):
    p0, p1, p2, p3 = parts
    g = math.exp(-c * c)
    even = g * p0 + (g * c * c) * p2
    odd = (g * c) * p1 + (g * c * c * c) * p3
    return even - odd, even + odd


def masks():
    lane = lax.broadcasted_iota(jnp.int32, (ROWS, LANES), 1)
    row = lax.broadcasted_iota(jnp.int32, (ROWS, LANES), 0)
    return lane, row


def from_y(f, step, lane):
    turned = pltpu.roll(f, (step * NZ) % LANES, 1)
    other = pltpu.roll(turned, ROWS // 2, 0)
    inside = (lane >= NZ) if step > 0 else (lane < LANES - NZ)
    return jnp.where(inside, turned, other)


def from_z(f, step, lane):
    near = pltpu.roll(f, step % LANES, 1)
    wrapped = pltpu.roll(f, (-step * (NZ - 1)) % LANES, 1)
    inside = (lane % NZ != 0) if step > 0 else (lane % NZ != NZ - 1)
    return jnp.where(inside, near, wrapped)


def transport_kernel(
    nvel, nspace, groups,
    f_hbm, m_hbm, pore_hbm, rate_hbm,
    g_ref, mnew_ref, corr_ref,
    f_ref, h_ref, m_ref, pore_ref, rate_ref, fsend, hsend, frecv, hrecv,
    acc, mrecv, pore_ext, change_ext,
    in_sem, small_sem, fs_sem, fr_sem, hs_sem, hr_sem, ms_sem, mr_sem, ps_sem, pr_sem, cs_sem, cr_sem,
):
    vel = lax.axis_index("vel")
    space = lax.axis_index("space")
    right = lax.rem(space + 1, nspace)
    left = lax.rem(space + nspace - 1, nspace)
    chunks = groups * 2
    positive = vel * 2 >= nvel
    target = jnp.where(positive, right, left)
    volume = (2.0 * extent) ** 3 / (VX * VY * VZ) / math.pi**1.5

    def load(c):
        rows = pl.ds(c * (CHUNK * ROWS), CHUNK * ROWS)
        return pltpu.make_async_copy(f_hbm.at[rows], f_ref.at[rows], in_sem.at[c])

    small = [
        pltpu.make_async_copy(src, dst, small_sem.at[n])
        for n, (src, dst) in enumerate(
            ((m_hbm, m_ref), (pore_hbm, pore_ref), (rate_hbm, rate_ref))
        )
    ]
    for c in range(chunks):
        load(c).start()
    for copy in small:
        copy.start()

    barrier = pltpu.get_barrier_semaphore()
    for other in (left, right):
        pl.semaphore_signal(barrier, inc=1, device_id={"space": other}, device_id_type=MESH)
    for d in range(1, nvel):
        pl.semaphore_signal(
            barrier, inc=1, device_id={"vel": lax.rem(vel + d, nvel)}, device_id_type=MESH
        )

    lane, row = masks()
    plane = lax.rem(row, ROWS // 2)
    for copy in small:
        copy.wait()
    pore = pore_ref[...].astype(jnp.float32)
    pore_ext[1] = pore
    edge = jnp.where(positive, 0, ROWS // 2 - 1)
    at_edge = jnp.where(plane == edge, 1.0, 0.0)
    off_edge = 1.0 - at_edge
    acc[...] = jnp.zeros_like(acc)
    fields = [m_ref[pl.ds(m * ROWS, ROWS), :] for m in range(NMOM)]

    def upwind_x(f):
        return jnp.where(positive, pltpu.roll(f, 1, 0), pltpu.roll(f, ROWS - 1, 0))

    def pack(src, base):
        lastp = src[pl.ds(base + ROWS // 2 - 1, ROWS, stride=ROWS // 2), :]
        firstp = src[pl.ds(base, ROWS, stride=ROWS // 2), :]
        return jnp.where(positive, lastp, firstp)

    def pack_chunk(src, dst, c):
        for t in range(CHUNK // 4):
            base = pl.multiple_of(c * (CHUNK * ROWS), ROWS) + t * 4 * ROWS
            dst[pl.ds(pl.multiple_of(c * (CHUNK * 2), ROWS) + t * ROWS, ROWS), :] = pack(src, base)

    def send(src, dst, s_sem, r_sem, c):
        rows = pl.ds(c * (CHUNK * 2), CHUNK * 2)
        return pltpu.make_async_remote_copy(
            src_ref=src.at[rows], dst_ref=dst.at[rows],
            send_sem=s_sem.at[c], recv_sem=r_sem.at[c],
            device_id={"space": target}, device_id_type=MESH,
        )

    def edges(src, dst, s_sem, r_sem):
        return [
            pltpu.make_async_remote_copy(
                src_ref=src.at[1], dst_ref=dst.at[2 * (1 - s)],
                send_sem=s_sem.at[s], recv_sem=r_sem.at[s],
                device_id={"space": (left, right)[s]}, device_id_type=MESH,
            )
            for s in range(2)
        ]

    def sweep(f, src, w, amask, ab, ac, bstep, cstep):
        total = src + amask * upwind_x(f)
        total = total + ab * from_y(f, bstep, lane)
        total = total + ac * from_z(f, cstep, lane)
        return w * total

    def node_ab(group, half, jj):
        a = node(vel * groups + group, VX)
        b = node(half * HALF + jj, VY)
        return a, b

    def first_chunk(c, group, half):
        bstep = 1 if half else -1

        def body(jj, carry):
            a, b = node_ab(group, half, jj)
            abs_a, abs_b = jnp.abs(a), jnp.abs(b)
            parts = poly_parts(fields, a, b)
            amask = abs_a * off_edge
            base = (c * HALF + jj) * (VZ * ROWS)
            for k in range(VZ // 2, VZ):
                cv = node_c(k)
                src = poly_pair(parts, cv)
                w = pore / (jnp.full((ROWS, LANES), 1.0 + abs_a + abs_b, jnp.float32) + cv)
                for sign in range(2):
                    kk = k if sign else VZ - 1 - k
                    rows = pl.ds(pl.multiple_of(base, ROWS) + kk * ROWS, ROWS)
                    f = f_ref[rows, :]
                    h_ref[rows, :] = sweep(
                        f, src[sign], w, amask, abs_b, cv, bstep, 1 if sign else -1
                    )
            return carry

        lax.fori_loop(0, HALF, body, 0)

    def second_chunk(c, group, half):
        bstep = 1 if half else -1

        def body(jj, carry):
            a, b = node_ab(group, half, jj)
            abs_a, abs_b = jnp.abs(a), jnp.abs(b)
            parts = poly_parts(fields, a, b)
            amask = abs_a * off_edge
            aedge = abs_a * at_edge
            base = (c * HALF + jj) * (VZ * ROWS)
            hbase = (c * HALF + jj) * (VZ * 2)
            s0 = s1 = s2 = s3 = None
            for k in range(VZ // 2, VZ):
                cv = node_c(k)
                src = poly_pair(parts, cv)
                w = pore / (jnp.full((ROWS, LANES), 1.0 + abs_a + abs_b, jnp.float32) + cv)
                wa = w * aedge
                got = []
                for sign in range(2):
                    kk = k if sign else VZ - 1 - k
                    rows = pl.ds(pl.multiple_of(base, ROWS) + kk * ROWS, ROWS)

                    def halo(ref):
                        at = pl.multiple_of(hbase, ROWS) + kk * 2
                        lower = jnp.broadcast_to(ref[pl.ds(at, 1), :], (ROWS, LANES))
                        upper = jnp.broadcast_to(ref[pl.ds(at + 1, 1), :], (ROWS, LANES))
                        return jnp.where(row < ROWS // 2, lower, upper)

                    h = h_ref[rows, :] + wa * halo(frecv)
                    total = sweep(h, src[sign], w, amask, abs_b, cv, bstep, 1 if sign else -1)
                    total = total + wa * halo(hrecv)
                    g_ref[rows, :] = total
                    got.append(total)
                u = got[1] + got[0]
                d = got[1] - got[0]
                if s0 is None:
                    s0, s1, s2, s3 = u, cv * d, (cv * cv) * u, (cv**3) * d
                else:
                    s0, s1 = s0 + u, s1 + cv * d
                    s2, s3 = s2 + (cv * cv) * u, s3 + (cv**3) * d
            q = a * a + b * b
            heat = (q - 2.5) * s0 + s2
            terms = (
                s0, a * s0, b * s0, s1, (q - 1.5) * s0 + s2,
                a * heat, b * heat, (q - 2.5) * s1 + s3, (a * b) * s0, b * s1,
            )
            for m, term in enumerate(terms):
                rows = pl.ds(m * ROWS, ROWS)
                acc[rows, :] = acc[rows, :] + term
            return carry

        lax.fori_loop(0, HALF, body, 0)

    def prepare(c, carry):
        load(c).wait()
        pack_chunk(f_ref, fsend, c)
        return carry

    lax.fori_loop(0, chunks, prepare, 0)

    pl.semaphore_wait(barrier, nvel + 1)

    def send_first(c, carry):
        send(fsend, frecv, fs_sem, fr_sem, c).start()
        return carry

    lax.fori_loop(0, chunks, send_first, 0)
    pores = edges(pore_ext, pore_ext, ps_sem, pr_sem)
    for copy in pores:
        copy.start()

    def phase_one(group, carry):
        for half in range(2):
            c = group * 2 + half
            first_chunk(c, group, half)
            pack_chunk(h_ref, hsend, c)
            send(hsend, hrecv, hs_sem, hr_sem, c).start()
        return carry

    lax.fori_loop(0, groups, phase_one, 0)

    def phase_two(group, carry):
        for half in range(2):
            c = group * 2 + half
            send(fsend, frecv, fs_sem, fr_sem, c).wait_recv()
            send(hsend, hrecv, hs_sem, hr_sem, c).wait_recv()
            second_chunk(c, group, half)
        return carry

    lax.fori_loop(0, groups, phase_two, 0)

    mrecv[vel] = acc[...] * volume

    def moment_copy(d, slot):
        return pltpu.make_async_remote_copy(
            src_ref=mrecv.at[vel], dst_ref=mrecv.at[slot],
            send_sem=ms_sem.at[d - 1], recv_sem=mr_sem.at[slot],
            device_id={"vel": lax.rem(vel + d, nvel)}, device_id_type=MESH,
        )

    for d in range(1, nvel):
        moment_copy(d, vel).start()
    for d in range(1, nvel):
        moment_copy(d, lax.rem(vel + d, nvel)).wait_recv()
    total = mrecv[0]
    for s in range(1, nvel):
        total = total + mrecv[s]
    mnew_ref[...] = total
    change_ext[1] = total - m_ref[...]
    changes = edges(change_ext, change_ext, cs_sem, cr_sem)
    for copy in changes:
        copy.start()
    for copy in pores:
        copy.wait()
    for copy in changes:
        copy.wait_recv()

    first = plane == 0
    final = plane == ROWS // 2 - 1
    up = ROWS - ROWS // 2 + 1
    down = ROWS // 2 - 1
    porous = [pore_ext[s] for s in range(3)]

    for m in range(NMOM):
        rows = pl.ds(m * ROWS, ROWS)
        scale = 1.0 / jnp.full((ROWS, LANES), rate_ref[m] + 6.0, jnp.float32)
        forcing = [change_ext[s, rows, :] for s in range(3)]
        gain = [porous[s] * scale for s in range(3)]
        value = [gain[s] * forcing[s] for s in range(3)]
        for step in range(SWEEPS - 1):
            fresh = list(value)
            for s in (range(3) if step < SWEEPS - 2 else (1,)):
                v = value[s]
                before = pltpu.roll(v, 1, 0)
                after = pltpu.roll(v, ROWS - 1, 0)
                if s > 0:
                    before = jnp.where(first, pltpu.roll(value[s - 1], up, 0), before)
                if s < 2:
                    after = jnp.where(final, pltpu.roll(value[s + 1], down, 0), after)
                beside = from_y(v, 1, lane) + from_y(v, -1, lane)
                beside = beside + from_z(v, 1, lane) + from_z(v, -1, lane)
                fresh[s] = gain[s] * (forcing[s] + (before + after + beside))
            value = fresh
        mnew_ref[rows, :] = mnew_ref[rows, :] + value[1]
        corr_ref[rows, :] = pore * value[1]

    for copy in changes:
        copy.wait_send()
    for d in range(1, nvel):
        moment_copy(d, vel).wait_send()

    def finish(c, carry):
        send(fsend, frecv, fs_sem, fr_sem, c).wait_send()
        send(hsend, hrecv, hs_sem, hr_sem, c).wait_send()
        return carry

    lax.fori_loop(0, chunks, finish, 0)


def group_parts(m, a):
    k = coefficients
    a = jnp.full((ROWS, LANES), a, jnp.float32)
    a2 = a * a
    weight = jnp.exp(-a2)
    bb = k[4] * m[4] + (k[5] * a) * m[5]
    one = k[0] * m[0] + (k[1] * a) * m[1] + (k[4] * (a2 - 1.5)) * m[4] + (k[5] * a * (a2 - 2.5)) * m[5]
    b1 = k[2] * m[2] + (k[6] * (a2 - 2.5)) * m[6] + (k[8] * a) * m[8]
    c1 = k[3] * m[3] + (k[7] * (a2 - 2.5)) * m[7]
    return [weight * x for x in (one, b1, bb, k[6] * m[6], c1, k[9] * m[9], k[7] * m[7])]


def pair_parts(parts, b):
    one, b1, bb, bbb, c1, cb, cbb = parts
    g = math.exp(-b * b)
    p0e, p0o = g * one + (g * b * b) * bb, (g * b) * b1 + (g * b**3) * bbb
    p1e, p1o = g * c1 + (g * b * b) * cbb, (g * b) * cb
    p2e, p2o = g * bb, (g * b) * bbb
    p3 = g * cbb
    return (
        (p0e - p0o, p1e - p1o, p2e - p2o, p3),
        (p0e + p0o, p1e + p1o, p2e + p2o, p3),
    )


def node_b(j):
    return -extent + (j + 0.5) * (2.0 * extent / VY)


def lift_kernel(groups, half_ref, corr_ref, mnew_ref, out_hbm, mout_hbm, stage, sem, msem):
    vel = lax.axis_index("vel")
    size = VY * VZ * ROWS
    moments = pltpu.make_async_copy(mnew_ref, mout_hbm, msem)
    moments.start()

    def store(g):
        rows = pl.ds(g * size, size)
        return pltpu.make_async_copy(stage.at[rows], out_hbm.at[rows], sem.at[g])

    def body(g, carry):
        fields = [corr_ref[pl.ds(m * ROWS, ROWS), :] for m in range(NMOM)]
        parts = group_parts(fields, node(vel * groups + g, VX))
        base = pl.multiple_of(g * size, ROWS)
        for j in range(HALF, VY):
            both = pair_parts(parts, node_b(j))
            for bsign in range(2):
                jj = j if bsign else VY - 1 - j
                for k in range(VZ // 2, VZ):
                    lifted = poly_pair(both[bsign], node_c(k))
                    for sign in range(2):
                        kk = k if sign else VZ - 1 - k
                        rows = pl.ds(base + (jj * VZ + kk) * ROWS, ROWS)
                        stage[rows, :] = half_ref[rows, :] + lifted[sign]
        store(g).start()
        return carry

    lax.fori_loop(0, groups, body, 0)

    def finish(g, carry):
        store(g).wait()
        return carry

    lax.fori_loop(0, groups, finish, 0)
    moments.wait()


def to_rows(x):
    lead, thickness, cells = x.shape
    parts = cells // LANES
    return x.reshape(lead, thickness, parts, LANES).transpose(0, 2, 1, 3).reshape(-1, LANES)


def from_rows(x, lead, thickness, cells):
    parts = cells // LANES
    return x.reshape(lead, parts, thickness, LANES).transpose(0, 2, 1, 3).reshape(lead, thickness, cells)


def body(nvel, nspace, distribution, moments_old, pore_mask, synthetic_rate):
    velocities, thickness, cells = distribution.shape
    groups = velocities // (VY * VZ)
    assert thickness * cells == ROWS * LANES and nvel % 2 == 0 and thickness >= SWEEPS - 1
    rows = to_rows(distribution)
    old = to_rows(moments_old)
    pore = to_rows(pore_mask[None])
    chunks = groups * 2
    total = velocities * ROWS
    vmem = pl.BlockSpec(memory_space=pltpu.VMEM)
    hbm = pl.BlockSpec(memory_space=pltpu.HBM)
    f32 = jnp.float32
    dma = pltpu.SemaphoreType.DMA
    half, moments_new, correction = pl.pallas_call(
        functools.partial(transport_kernel, nvel, nspace, groups),
        out_shape=(
            jax.ShapeDtypeStruct((total, LANES), f32),
            jax.ShapeDtypeStruct((NMOM * ROWS, LANES), f32),
            jax.ShapeDtypeStruct((NMOM * ROWS, LANES), f32),
        ),
        in_specs=[hbm] * 4,
        out_specs=(vmem,) * 3,
        scratch_shapes=[
            pltpu.VMEM((total, LANES), f32),
            pltpu.VMEM((total, LANES), f32),
            pltpu.VMEM((NMOM * ROWS, LANES), f32),
            pltpu.VMEM((ROWS, LANES), jnp.int32),
            pltpu.SMEM((NMOM,), f32),
            pltpu.VMEM((velocities * 2, LANES), f32),
            pltpu.VMEM((velocities * 2, LANES), f32),
            pltpu.VMEM((velocities * 2, LANES), f32),
            pltpu.VMEM((velocities * 2, LANES), f32),
            pltpu.VMEM((NMOM * ROWS, LANES), f32),
            pltpu.VMEM((nvel, NMOM * ROWS, LANES), f32),
            pltpu.VMEM((3, ROWS, LANES), f32),
            pltpu.VMEM((3, NMOM * ROWS, LANES), f32),
            dma((chunks,)), dma((3,)), dma((chunks,)), dma((chunks,)), dma((chunks,)), dma((chunks,)),
            dma((nvel - 1,)), dma((nvel,)), dma((2,)), dma((2,)), dma((2,)), dma((2,)),
        ],
        compiler_params=pltpu.CompilerParams(
            collective_id=0, has_side_effects=True, vmem_limit_bytes=24 * 1024 * 1024
        ),
        name="transport",
    )(*(pltpu.with_memory_space_constraint(x, pltpu.HBM) for x in (rows, old, pore, synthetic_rate)))
    new, moments_out = pl.pallas_call(
        functools.partial(lift_kernel, groups),
        out_shape=(
            jax.ShapeDtypeStruct((total, LANES), f32),
            jax.ShapeDtypeStruct((NMOM * ROWS, LANES), f32),
        ),
        in_specs=[vmem] * 3,
        out_specs=(hbm,) * 2,
        scratch_shapes=[pltpu.VMEM((total, LANES), f32), dma((groups,)), dma(())],
        compiler_params=pltpu.CompilerParams(vmem_limit_bytes=12 * 1024 * 1024),
        name="lift",
    )(half, correction, moments_new)
    return (
        from_rows(new, velocities, thickness, cells),
        from_rows(moments_out, NMOM, thickness, cells),
    )


def solution(mesh):
    placed = (P("vel", "space", None), P(None, "space", None), P("space", None), P())
    return jax.shard_map(
        functools.partial(body, mesh.shape["vel"], mesh.shape["space"]),
        mesh=mesh,
        in_specs=placed,
        out_specs=(P("vel", "space", None), P(None, "space", None)),
        check_vma=False,
    )
```

```python
import functools
import math

import jax
import jax.numpy as jnp
from jax import lax
from jax.experimental import pallas as pl
from jax.experimental.pallas import tpu as pltpu
from jax.sharding import PartitionSpec as P

VX = 16
VY = 12
VZ = 12
NY = 16
NZ = 16
TSWEEPS = 2
SWEEPS = 5

extent = 3.0
coefficients = (1.0, 2.0, 2.0, 2.0, 0.6667, 0.8, 0.8, 0.8, 2.0, 2.0)
NMOM = len(coefficients)
LANES = 128
ROWS = 8
HALF = VY // 2
CHUNK = HALF * VZ
MESH = pl.DeviceIdType.MESH


def node(index, count):
    return -extent + (index.astype(jnp.float32) + 0.5) * (2.0 * extent / count)


def node_c(k):
    return -extent + (k + 0.5) * (2.0 * extent / VZ)


def poly_parts(fields, a, b):
    k = coefficients
    q = a * a + b * b
    m = fields
    p2 = k[4] * m[4] + (k[5] * a) * m[5] + (k[6] * b) * m[6]
    p0 = (
        k[0] * m[0]
        + (k[1] * a) * m[1]
        + (k[2] * b) * m[2]
        + (k[4] * (q - 1.5)) * m[4]
        + (k[5] * a * (q - 2.5)) * m[5]
        + (k[6] * b * (q - 2.5)) * m[6]
        + (k[8] * a * b) * m[8]
    )
    p1 = k[3] * m[3] + (k[7] * (q - 2.5)) * m[7] + (k[9] * b) * m[9]
    p3 = k[7] * m[7]
    weight = jnp.exp(jnp.full((ROWS, LANES), -q, jnp.float32))
    return weight * p0, weight * p1, weight * p2, weight * p3


def poly_pair(parts, c):
    p0, p1, p2, p3 = parts
    g = math.exp(-c * c)
    even = g * p0 + (g * c * c) * p2
    odd = (g * c) * p1 + (g * c * c * c) * p3
    return even - odd, even + odd


def masks():
    lane = lax.broadcasted_iota(jnp.int32, (ROWS, LANES), 1)
    row = lax.broadcasted_iota(jnp.int32, (ROWS, LANES), 0)
    return lane, row


def from_y(f, step, lane):
    turned = pltpu.roll(f, (step * NZ) % LANES, 1)
    other = pltpu.roll(turned, ROWS // 2, 0)
    inside = (lane >= NZ) if step > 0 else (lane < LANES - NZ)
    return jnp.where(inside, turned, other)


def from_z(f, step, lane):
    near = pltpu.roll(f, step % LANES, 1)
    wrapped = pltpu.roll(f, (-step * (NZ - 1)) % LANES, 1)
    inside = (lane % NZ != 0) if step > 0 else (lane % NZ != NZ - 1)
    return jnp.where(inside, near, wrapped)


def transport_kernel(
    nvel, nspace, groups,
    f_hbm, m_hbm, pore_hbm, rate_hbm,
    g_ref, mnew_ref, corr_ref,
    f_ref, h_ref, m_ref, pore_ref, rate_ref, fsend, hsend, frecv, hrecv,
    acc, mrecv, pore_ext, change_ext,
    in_sem, small_sem, fs_sem, fr_sem, hs_sem, hr_sem, ms_sem, mr_sem, ps_sem, pr_sem, cs_sem, cr_sem,
):
    vel = lax.axis_index("vel")
    space = lax.axis_index("space")
    right = lax.rem(space + 1, nspace)
    left = lax.rem(space + nspace - 1, nspace)
    chunks = groups * 2
    positive = vel * 2 >= nvel
    target = jnp.where(positive, right, left)
    volume = (2.0 * extent) ** 3 / (VX * VY * VZ) / math.pi**1.5

    def load(c):
        rows = pl.ds(c * (CHUNK * ROWS), CHUNK * ROWS)
        return pltpu.make_async_copy(f_hbm.at[rows], f_ref.at[rows], in_sem.at[c])

    small = [
        pltpu.make_async_copy(src, dst, small_sem.at[n])
        for n, (src, dst) in enumerate(
            ((m_hbm, m_ref), (pore_hbm, pore_ref), (rate_hbm, rate_ref))
        )
    ]
    for c in range(chunks):
        load(c).start()
    for copy in small:
        copy.start()

    barrier = pltpu.get_barrier_semaphore()
    for other in (left, right):
        pl.semaphore_signal(barrier, inc=1, device_id={"space": other}, device_id_type=MESH)
    for d in range(1, nvel):
        pl.semaphore_signal(
            barrier, inc=1, device_id={"vel": lax.rem(vel + d, nvel)}, device_id_type=MESH
        )

    lane, row = masks()
    plane = lax.rem(row, ROWS // 2)
    edge = jnp.where(positive, 0, ROWS // 2 - 1)
    at_edge = jnp.where(plane == edge, 1.0, 0.0)
    off_edge = 1.0 - at_edge
    acc[...] = jnp.zeros_like(acc)

    def upwind_x(f):
        return jnp.where(positive, pltpu.roll(f, 1, 0), pltpu.roll(f, ROWS - 1, 0))

    def pack(src, base):
        lastp = src[pl.ds(base + ROWS // 2 - 1, ROWS, stride=ROWS // 2), :]
        firstp = src[pl.ds(base, ROWS, stride=ROWS // 2), :]
        return jnp.where(positive, lastp, firstp)

    def pack_chunk(src, dst, c):
        for t in range(CHUNK // 4):
            base = pl.multiple_of(c * (CHUNK * ROWS), ROWS) + t * 4 * ROWS
            dst[pl.ds(pl.multiple_of(c * (CHUNK * 2), ROWS) + t * ROWS, ROWS), :] = pack(src, base)

    def send(src, dst, s_sem, r_sem, c):
        rows = pl.ds(c * (CHUNK * 2), CHUNK * 2)
        return pltpu.make_async_remote_copy(
            src_ref=src.at[rows], dst_ref=dst.at[rows],
            send_sem=s_sem.at[c], recv_sem=r_sem.at[c],
            device_id={"space": target}, device_id_type=MESH,
        )

    def edges(src, dst, s_sem, r_sem):
        return [
            pltpu.make_async_remote_copy(
                src_ref=src.at[1], dst_ref=dst.at[2 * (1 - s)],
                send_sem=s_sem.at[s], recv_sem=r_sem.at[s],
                device_id={"space": (left, right)[s]}, device_id_type=MESH,
            )
            for s in range(2)
        ]

    def sweep(f, src, w, amask, ab, ac, bstep, cstep):
        total = src + amask * upwind_x(f)
        total = total + ab * from_y(f, bstep, lane)
        total = total + ac * from_z(f, cstep, lane)
        return w * total

    def node_ab(group, half, jj):
        a = node(vel * groups + group, VX)
        b = node(half * HALF + jj, VY)
        return a, b

    def first_chunk(c, group, half):
        bstep = 1 if half else -1

        def body(jj, carry):
            a, b = node_ab(group, half, jj)
            abs_a, abs_b = jnp.abs(a), jnp.abs(b)
            parts = poly_parts(fields, a, b)
            amask = abs_a * off_edge
            base = (c * HALF + jj) * (VZ * ROWS)
            for k in range(VZ // 2, VZ):
                cv = node_c(k)
                src = poly_pair(parts, cv)
                w = pore / (jnp.full((ROWS, LANES), 1.0 + abs_a + abs_b, jnp.float32) + cv)
                for sign in range(2):
                    kk = k if sign else VZ - 1 - k
                    rows = pl.ds(pl.multiple_of(base, ROWS) + kk * ROWS, ROWS)
                    f = f_ref[rows, :]
                    h_ref[rows, :] = sweep(
                        f, src[sign], w, amask, abs_b, cv, bstep, 1 if sign else -1
                    )
            return carry

        lax.fori_loop(0, HALF, body, 0)

    def second_chunk(c, group, half):
        bstep = 1 if half else -1

        def body(jj, carry):
            a, b = node_ab(group, half, jj)
            abs_a, abs_b = jnp.abs(a), jnp.abs(b)
            parts = poly_parts(fields, a, b)
            amask = abs_a * off_edge
            aedge = abs_a * at_edge
            base = (c * HALF + jj) * (VZ * ROWS)
            hbase = (c * HALF + jj) * (VZ * 2)
            s0 = s1 = s2 = s3 = None
            for k in range(VZ // 2, VZ):
                cv = node_c(k)
                src = poly_pair(parts, cv)
                w = pore / (jnp.full((ROWS, LANES), 1.0 + abs_a + abs_b, jnp.float32) + cv)
                wa = w * aedge
                got = []
                for sign in range(2):
                    kk = k if sign else VZ - 1 - k
                    rows = pl.ds(pl.multiple_of(base, ROWS) + kk * ROWS, ROWS)

                    def halo(ref):
                        at = pl.multiple_of(hbase, ROWS) + kk * 2
                        lower = jnp.broadcast_to(ref[pl.ds(at, 1), :], (ROWS, LANES))
                        upper = jnp.broadcast_to(ref[pl.ds(at + 1, 1), :], (ROWS, LANES))
                        return jnp.where(row < ROWS // 2, lower, upper)

                    h = h_ref[rows, :] + wa * halo(frecv)
                    total = sweep(h, src[sign], w, amask, abs_b, cv, bstep, 1 if sign else -1)
                    total = total + wa * halo(hrecv)
                    g_ref[rows, :] = total
                    got.append(total)
                u = got[1] + got[0]
                d = got[1] - got[0]
                if s0 is None:
                    s0, s1, s2, s3 = u, cv * d, (cv * cv) * u, (cv**3) * d
                else:
                    s0, s1 = s0 + u, s1 + cv * d
                    s2, s3 = s2 + (cv * cv) * u, s3 + (cv**3) * d
            q = a * a + b * b
            heat = (q - 2.5) * s0 + s2
            terms = (
                s0, a * s0, b * s0, s1, (q - 1.5) * s0 + s2,
                a * heat, b * heat, (q - 2.5) * s1 + s3, (a * b) * s0, b * s1,
            )
            for m, term in enumerate(terms):
                rows = pl.ds(m * ROWS, ROWS)
                acc[rows, :] = acc[rows, :] + term
            return carry

        lax.fori_loop(0, HALF, body, 0, unroll=3)

    def send_first(c, carry):
        load(c).wait()
        pack_chunk(f_ref, fsend, c)
        send(fsend, frecv, fs_sem, fr_sem, c).start()
        return carry

    load(0).wait()
    pack_chunk(f_ref, fsend, 0)
    pl.semaphore_wait(barrier, nvel + 1)
    send(fsend, frecv, fs_sem, fr_sem, 0).start()
    lax.fori_loop(1, chunks, send_first, 0)

    for copy in small:
        copy.wait()
    pore = pore_ref[...].astype(jnp.float32)
    pore_ext[1] = pore
    fields = [m_ref[pl.ds(m * ROWS, ROWS), :] for m in range(NMOM)]
    pores = edges(pore_ext, pore_ext, ps_sem, pr_sem)
    for copy in pores:
        copy.start()

    def phase_one(group, carry):
        for half in range(2):
            c = group * 2 + half
            first_chunk(c, group, half)
            pack_chunk(h_ref, hsend, c)
            send(hsend, hrecv, hs_sem, hr_sem, c).start()
        return carry

    lax.fori_loop(0, groups, phase_one, 0)

    def phase_two(group, carry):
        for half in range(2):
            c = group * 2 + half
            send(fsend, frecv, fs_sem, fr_sem, c).wait_recv()
            send(hsend, hrecv, hs_sem, hr_sem, c).wait_recv()
            second_chunk(c, group, half)
        return carry

    lax.fori_loop(0, groups, phase_two, 0)

    mrecv[vel] = acc[...] * volume

    def moment_copy(d, slot):
        return pltpu.make_async_remote_copy(
            src_ref=mrecv.at[vel], dst_ref=mrecv.at[slot],
            send_sem=ms_sem.at[d - 1], recv_sem=mr_sem.at[slot],
            device_id={"vel": lax.rem(vel + d, nvel)}, device_id_type=MESH,
        )

    for d in range(1, nvel):
        moment_copy(d, vel).start()
    for d in range(1, nvel):
        moment_copy(d, lax.rem(vel + d, nvel)).wait_recv()
    total = mrecv[0]
    for s in range(1, nvel):
        total = total + mrecv[s]
    mnew_ref[...] = total
    change_ext[1] = total - m_ref[...]
    changes = edges(change_ext, change_ext, cs_sem, cr_sem)
    for copy in changes:
        copy.start()
    for copy in pores:
        copy.wait()
    for copy in changes:
        copy.wait_recv()

    first = plane == 0
    final = plane == ROWS // 2 - 1
    up = ROWS - ROWS // 2 + 1
    down = ROWS // 2 - 1
    porous = [pore_ext[s] for s in range(3)]

    for m in range(NMOM):
        rows = pl.ds(m * ROWS, ROWS)
        scale = 1.0 / jnp.full((ROWS, LANES), rate_ref[m] + 6.0, jnp.float32)
        forcing = [change_ext[s, rows, :] for s in range(3)]
        gain = [porous[s] * scale for s in range(3)]
        value = [gain[s] * forcing[s] for s in range(3)]
        for step in range(SWEEPS - 1):
            fresh = list(value)
            for s in (range(3) if step < SWEEPS - 2 else (1,)):
                v = value[s]
                before = pltpu.roll(v, 1, 0)
                after = pltpu.roll(v, ROWS - 1, 0)
                if s > 0:
                    before = jnp.where(first, pltpu.roll(value[s - 1], up, 0), before)
                if s < 2:
                    after = jnp.where(final, pltpu.roll(value[s + 1], down, 0), after)
                beside = from_y(v, 1, lane) + from_y(v, -1, lane)
                beside = beside + from_z(v, 1, lane) + from_z(v, -1, lane)
                fresh[s] = gain[s] * (forcing[s] + (before + after + beside))
            value = fresh
        mnew_ref[rows, :] = mnew_ref[rows, :] + value[1]
        corr_ref[rows, :] = pore * value[1]

    for copy in changes:
        copy.wait_send()
    for d in range(1, nvel):
        moment_copy(d, vel).wait_send()

    def finish(c, carry):
        send(fsend, frecv, fs_sem, fr_sem, c).wait_send()
        send(hsend, hrecv, hs_sem, hr_sem, c).wait_send()
        return carry

    lax.fori_loop(0, chunks, finish, 0)


def group_parts(m, a):
    k = coefficients
    a = jnp.full((ROWS, LANES), a, jnp.float32)
    a2 = a * a
    weight = jnp.exp(-a2)
    bb = k[4] * m[4] + (k[5] * a) * m[5]
    one = k[0] * m[0] + (k[1] * a) * m[1] + (k[4] * (a2 - 1.5)) * m[4] + (k[5] * a * (a2 - 2.5)) * m[5]
    b1 = k[2] * m[2] + (k[6] * (a2 - 2.5)) * m[6] + (k[8] * a) * m[8]
    c1 = k[3] * m[3] + (k[7] * (a2 - 2.5)) * m[7]
    return [weight * x for x in (one, b1, bb, k[6] * m[6], c1, k[9] * m[9], k[7] * m[7])]


def pair_parts(parts, b):
    one, b1, bb, bbb, c1, cb, cbb = parts
    g = math.exp(-b * b)
    p0e, p0o = g * one + (g * b * b) * bb, (g * b) * b1 + (g * b**3) * bbb
    p1e, p1o = g * c1 + (g * b * b) * cbb, (g * b) * cb
    p2e, p2o = g * bb, (g * b) * bbb
    p3 = g * cbb
    return (
        (p0e - p0o, p1e - p1o, p2e - p2o, p3),
        (p0e + p0o, p1e + p1o, p2e + p2o, p3),
    )


def node_b(j):
    return -extent + (j + 0.5) * (2.0 * extent / VY)


def lift_kernel(groups, half_ref, corr_ref, mnew_ref, out_hbm, mout_hbm, stage, sem, msem):
    vel = lax.axis_index("vel")
    size = VY * VZ * ROWS
    moments = pltpu.make_async_copy(mnew_ref, mout_hbm, msem)
    moments.start()

    def store(g):
        rows = pl.ds(g * size, size)
        return pltpu.make_async_copy(stage.at[rows], out_hbm.at[rows], sem.at[g])

    def body(g, carry):
        fields = [corr_ref[pl.ds(m * ROWS, ROWS), :] for m in range(NMOM)]
        parts = group_parts(fields, node(vel * groups + g, VX))
        base = pl.multiple_of(g * size, ROWS)
        for j in range(HALF, VY):
            both = pair_parts(parts, node_b(j))
            for bsign in range(2):
                jj = j if bsign else VY - 1 - j
                for k in range(VZ // 2, VZ):
                    lifted = poly_pair(both[bsign], node_c(k))
                    for sign in range(2):
                        kk = k if sign else VZ - 1 - k
                        rows = pl.ds(base + (jj * VZ + kk) * ROWS, ROWS)
                        stage[rows, :] = half_ref[rows, :] + lifted[sign]
        store(g).start()
        return carry

    lax.fori_loop(0, groups, body, 0)

    def finish(g, carry):
        store(g).wait()
        return carry

    lax.fori_loop(0, groups, finish, 0)
    moments.wait()


def to_rows(x):
    lead, thickness, cells = x.shape
    parts = cells // LANES
    return x.reshape(lead, thickness, parts, LANES).transpose(0, 2, 1, 3).reshape(-1, LANES)


def from_rows(x, lead, thickness, cells):
    parts = cells // LANES
    return x.reshape(lead, parts, thickness, LANES).transpose(0, 2, 1, 3).reshape(lead, thickness, cells)


def body(nvel, nspace, distribution, moments_old, pore_mask, synthetic_rate):
    velocities, thickness, cells = distribution.shape
    groups = velocities // (VY * VZ)
    assert thickness * cells == ROWS * LANES and nvel % 2 == 0 and thickness >= SWEEPS - 1
    rows = to_rows(distribution)
    old = to_rows(moments_old)
    pore = to_rows(pore_mask[None])
    chunks = groups * 2
    total = velocities * ROWS
    vmem = pl.BlockSpec(memory_space=pltpu.VMEM)
    hbm = pl.BlockSpec(memory_space=pltpu.HBM)
    f32 = jnp.float32
    dma = pltpu.SemaphoreType.DMA
    half, moments_new, correction = pl.pallas_call(
        functools.partial(transport_kernel, nvel, nspace, groups),
        out_shape=(
            jax.ShapeDtypeStruct((total, LANES), f32),
            jax.ShapeDtypeStruct((NMOM * ROWS, LANES), f32),
            jax.ShapeDtypeStruct((NMOM * ROWS, LANES), f32),
        ),
        in_specs=[hbm] * 4,
        out_specs=(vmem,) * 3,
        scratch_shapes=[
            pltpu.VMEM((total, LANES), f32),
            pltpu.VMEM((total, LANES), f32),
            pltpu.VMEM((NMOM * ROWS, LANES), f32),
            pltpu.VMEM((ROWS, LANES), jnp.int32),
            pltpu.SMEM((NMOM,), f32),
            pltpu.VMEM((velocities * 2, LANES), f32),
            pltpu.VMEM((velocities * 2, LANES), f32),
            pltpu.VMEM((velocities * 2, LANES), f32),
            pltpu.VMEM((velocities * 2, LANES), f32),
            pltpu.VMEM((NMOM * ROWS, LANES), f32),
            pltpu.VMEM((nvel, NMOM * ROWS, LANES), f32),
            pltpu.VMEM((3, ROWS, LANES), f32),
            pltpu.VMEM((3, NMOM * ROWS, LANES), f32),
            dma((chunks,)), dma((3,)), dma((chunks,)), dma((chunks,)), dma((chunks,)), dma((chunks,)),
            dma((nvel - 1,)), dma((nvel,)), dma((2,)), dma((2,)), dma((2,)), dma((2,)),
        ],
        compiler_params=pltpu.CompilerParams(
            collective_id=0, has_side_effects=True, vmem_limit_bytes=24 * 1024 * 1024
        ),
        name="transport",
    )(*(pltpu.with_memory_space_constraint(x, pltpu.HBM) for x in (rows, old, pore, synthetic_rate)))
    new, moments_out = pl.pallas_call(
        functools.partial(lift_kernel, groups),
        out_shape=(
            jax.ShapeDtypeStruct((total, LANES), f32),
            jax.ShapeDtypeStruct((NMOM * ROWS, LANES), f32),
        ),
        in_specs=[vmem] * 3,
        out_specs=(hbm,) * 2,
        scratch_shapes=[pltpu.VMEM((total, LANES), f32), dma((groups,)), dma(())],
        compiler_params=pltpu.CompilerParams(vmem_limit_bytes=12 * 1024 * 1024),
        name="lift",
    )(half, correction, moments_new)
    return (
        from_rows(new, velocities, thickness, cells),
        from_rows(moments_out, NMOM, thickness, cells),
    )


def solution(mesh):
    placed = (P("vel", "space", None), P(None, "space", None), P("space", None), P())
    return jax.shard_map(
        functools.partial(body, mesh.shape["vel"], mesh.shape["space"]),
        mesh=mesh,
        in_specs=placed,
        out_specs=(P("vel", "space", None), P(None, "space", None)),
        check_vma=False,
    )
```
